32 devices in a mesh: member: 4 (over x, core), grid: 8 (over z, y).
Axes of the slice: x: 2, y: 2, z: 4, core: 2. Of those that a mesh axis runs over, the one named last changes fastest.
Arguments:
- features: bfloat16 [4, 32, 512, 256], P('member', None, 'grid'), may hold values from -6 to 6
- perturbation: bfloat16 [4, 32, 512, 256], P('member', None, 'grid'), may hold values from -4 to 4
- target: bfloat16 [32, 32768], P(None, 'grid'), may hold values from -8 to 8
- head_weight: bfloat16 [256, 64], replicated, may hold values from -0.375 to 0.375
- head_bias: float32 [64], replicated, may hold values from -4 to 4
Outputs:
- hidden_grad: bfloat16 [4, 32, 512, 256], P('member', None, 'grid')
- head_grad: float32 [256, 64], P('grid')
The draws below stay inside these ranges and needn't reach their ends.
All inputs are finite; a program needn't handle non-finite values.
Results may differ from the reference program's by a relative error of at most 0.011.
Values may be sent and summed in bfloat16 or wider, within the bound.
A program may use at most 64 MiB of HBM per device.

```python
import jax
import jax.numpy as jnp
from jax import lax

CH = 64
HID = 256
ROWS = 32
MEMBERS = 4
NCOL = 512
N_MEMBER = 4


def with_spikes(array, stream_key, source, target, parts, factor):
    owner, partner = [(jnp.arange(array.shape[axis_at]) // (array.shape[axis_at] // parts)).reshape([-1 if axis == axis_at else 1 for axis in range(array.ndim)]) for axis_at in (source, target)]
    chosen = jax.random.permutation(stream_key, parts)[partner]
    strong = (owner == chosen) | (owner == (partner + parts // 2) % parts)
    return jnp.where(strong, factor * array, array)


def block_scale(own_key, extent, pieces, low, top_value):
    def one(axis_at, blocks):
        steps = jax.random.uniform(jax.random.fold_in(jax.random.fold_in(own_key, 6), axis_at), (blocks,), jnp.float32, low / len(pieces), top_value / len(pieces))
        return jnp.repeat(jnp.exp(steps), extent[axis_at] // blocks).reshape((-1,) + (1,) * (len(extent) - axis_at - 1))

    level = one(*pieces[0])
    for cut in pieces[1:]:
        level = level * one(*cut)
    return level


def scatter_about(own_key, dims, deviation, reach, shards=(), dtype=jnp.bfloat16):
    level = block_scale(own_key, dims, shards, -0.22, 0.18) if shards else 1.0
    drawn = jax.random.normal(own_key, dims, jnp.float32) * deviation * level
    return jnp.minimum(jnp.maximum(drawn, -reach), reach).astype(dtype)


def gaussian_with(key, shape, spread, bound, cuts, heavy, kind=jnp.bfloat16):
    array = spread * jax.random.normal(key, shape, jnp.float32)
    if cuts:
        array = array * block_scale(key, shape, cuts, -0.22, 0.18)
    return jnp.clip(with_spikes(array, jax.random.fold_in(key, 3), *heavy), -bound, bound).astype(kind)


def setup_inputs(seed: int = 0) -> dict:
    key_of = jax.random.split(jax.random.key(seed), 6)
    return {
        "features": gaussian_with(key_of[0], (MEMBERS, ROWS, NCOL, HID), 1.0, 6.0, ((0, 4), (2, 8)), (2, 3, 8, 2.0)),
        "perturbation": scatter_about(key_of[1], (MEMBERS, ROWS, NCOL, HID), 0.5, 4.0, ((0, 4), (2, 8))),
        "target": scatter_about(key_of[2], (ROWS, NCOL * CH), 1.5, 8.0, ((1, 8),)),
        "head_weight": scatter_about(key_of[3], (HID, CH), HID ** -0.5, 0.375),
        "head_bias": scatter_about(key_of[4], (CH,), 0.7, 4.0, (), jnp.float32),
    }


def smooth_sign(value):
    return value / jnp.sqrt(value * value + 0.01)

def reference(features, perturbation, target, head_weight, head_bias):
    weight_wide = head_weight.astype(jnp.float32)

    def forward(inputs):
        feature, jitter = inputs
        pre_act = feature.astype(jnp.float32) + jitter.astype(jnp.float32)
        activated = jax.nn.silu(pre_act).astype(jnp.bfloat16)
        pred = jnp.einsum('rch,hk->rck', activated.astype(jnp.float32), weight_wide) + head_bias
        return pred.astype(jnp.bfloat16)
    predictions = lax.map(forward, (features, perturbation))
    flat_pred = predictions.reshape(N_MEMBER, ROWS, NCOL * CH).astype(jnp.float32)
    flat_target = target.astype(jnp.float32)

    def grad_of(own_pred):

        def add_partner(partner, running):
            return running + smooth_sign(own_pred - flat_pred[partner])
        pair_sum = lax.fori_loop(0, N_MEMBER, add_partner, jnp.zeros(own_pred.shape, jnp.float32))
        return (smooth_sign(own_pred - flat_target) - pair_sum / (N_MEMBER - 1.0)).astype(jnp.bfloat16)
    pred_grads = lax.map(grad_of, flat_pred).reshape(N_MEMBER, ROWS, NCOL, CH)

    def backward(inputs):
        feature, jitter, pred_grad = inputs
        pre_act = feature.astype(jnp.float32) + jitter.astype(jnp.float32)
        activated = jax.nn.silu(pre_act).astype(jnp.bfloat16)
        grad_wide = pred_grad.astype(jnp.float32)
        act_grad = jnp.einsum('rck,hk->rch', grad_wide, weight_wide)
        gate_val = jax.nn.sigmoid(pre_act)
        hidden_grad = (act_grad * gate_val * (1.0 + pre_act * (1.0 - gate_val))).astype(jnp.bfloat16)
        head_part = jnp.einsum('rch,rck->hk', activated.astype(jnp.float32), grad_wide)
        return (hidden_grad, head_part)
    hidden_grad, head_parts = lax.map(backward, (features, perturbation, pred_grads))
    head_grad = lax.optimization_barrier(jnp.sum(head_parts, axis=0)) / (N_MEMBER * ROWS * NCOL * 1.0)
    return (hidden_grad, head_grad)
```

```python
import functools

import jax
import jax.numpy as jnp
from jax import lax
from jax.experimental import pallas as pl
from jax.experimental.pallas import tpu as pltpu
from jax.sharding import PartitionSpec as P

F32 = jnp.float32
BF16 = jnp.bfloat16
LANES = 128
CHUNKS = 4
TAIL = 2


def smooth_sign(value):
    return value * lax.rsqrt(value * value + 0.01)


def kernel(
    members,
    grid_count,
    features,
    perturbation,
    target,
    weight_t,
    bias,
    hidden_grad,
    head_grad,
    feat_buf,
    pert_buf,
    target_buf,
    target_cells,
    weight_pair,
    act_buf,
    gate_buf,
    preds,
    hidden_buf,
    head_acc,
    grid_send,
    grid_recv,
    member_sum,
    in_sem,
    target_sem,
    out_sem,
    pred_send_sem,
    pred_recv_sem,
    grid_send_sem,
    grid_recv_sem,
    member_send_sem,
    member_recv_sem,
):
    _, band_rows, columns, hidden = features.shape
    channels = weight_t.shape[0]
    half = columns // 2
    rows = band_rows // CHUNKS
    cells = rows * half
    chips = members // 2
    member = lax.axis_index("member")
    grid = lax.axis_index("grid")
    core = lax.rem(member, 2)
    chip = member // 2
    sibling = chip * 2 + 1 - core

    loads = []
    for k in range(CHUNKS):
        span = pl.ds(k * rows, rows)
        pair = []
        for which, (source, buffer) in enumerate(((features, feat_buf), (perturbation, pert_buf))):
            copy = pltpu.make_async_copy(source.at[0, span], buffer.at[k], in_sem.at[which, k])
            copy.start()
            pair.append(copy)
        loads.append(pair)
    target_load = pltpu.make_async_copy(target, target_buf, target_sem)
    target_load.start()

    barrier = pltpu.get_barrier_semaphore()
    for offset in range(1, members):
        pl.semaphore_signal(
            barrier,
            inc=1,
            device_id={"member": lax.rem(member + offset, members)},
            device_id_type=pl.DeviceIdType.MESH,
        )
    for offset in range(1, grid_count):
        pl.semaphore_signal(
            barrier,
            inc=1,
            device_id={"grid": lax.rem(grid + offset, grid_count)},
            device_id_type=pl.DeviceIdType.MESH,
        )

    zero = jnp.zeros((channels, hidden), BF16)
    weight_pair[:channels, :hidden] = weight_t[...]
    weight_pair[:channels, hidden:] = zero
    weight_pair[channels:, :hidden] = zero
    weight_pair[channels:, hidden:] = weight_t[...]
    bias_pair = jnp.concatenate([bias[...], bias[...]], axis=1)

    def member_copy(source, slot, k, device):
        return pltpu.make_async_remote_copy(
            src_ref=source,
            dst_ref=preds.at[slot[0], slot[1], k],
            send_sem=pred_send_sem.at[slot[0], slot[1], k],
            recv_sem=pred_recv_sem.at[slot[0], slot[1], k],
            device_id={"member": device},
            device_id_type=pl.DeviceIdType.MESH,
        )

    def forward(k):
        for copy in loads[k]:
            copy.wait()
        for side in range(2):
            cols = pl.ds(side * half, half)
            lanes = pl.ds(side * hidden, hidden)
            pre_act = feat_buf[k, :, cols, :].astype(F32) + pert_buf[k, :, cols, :].astype(F32)
            pre_act = pre_act.reshape(cells, hidden)
            gate = 0.5 + 0.5 * jnp.tanh(0.5 * pre_act)
            activated = pre_act * gate
            act_buf[k, :, lanes] = activated.astype(BF16)
            gate_buf[k, :, lanes] = gate + activated * (1.0 - gate)
        pred = lax.dot_general(
            act_buf[k], weight_pair[...], (((1,), (1,)), ((), ())), preferred_element_type=F32
        )
        preds[0, 0, k] = (pred + bias_pair).astype(BF16)

    own_copies = []
    sib_copies = []
    for k in range(CHUNKS):
        forward(k)
        if k == 0:
            pl.semaphore_wait(barrier, members + grid_count - 2)
        across = []
        for d in range(1, chips):
            to_chip = lax.rem(chip + chips - d, chips)
            copy = member_copy(preds.at[0, 0, k], (d, 0), k, to_chip * 2 + core)
            copy.start()
            across.append(copy)
        own_copies.append(across)
        copy = member_copy(preds.at[0, 0, k], (0, 1), k, sibling)
        copy.start()
        sib_copies.append(copy)

    target_load.wait()
    low = lax.broadcasted_iota(jnp.int32, (band_rows, LANES), 1) < channels
    for i in range(half // 2):
        first = target_buf[:, pl.ds(i * LANES, LANES)].astype(F32)
        second = target_buf[:, pl.ds((half // 2 + i) * LANES, LANES)].astype(F32)
        even = jnp.where(low, first, pltpu.roll(second, channels, 1))
        odd = jnp.where(low, pltpu.roll(first, channels, 1), second)
        target_cells[pl.ds(2 * i, band_rows, stride=half), :] = even
        target_cells[pl.ds(2 * i + 1, band_rows, stride=half), :] = odd

    def backward_scores(k):
        own = preds[0, 0, k].astype(F32)
        sib_copies[k].wait_recv()
        total = smooth_sign(own - preds[0, 1, k].astype(F32))
        for d in range(1, chips):
            total += smooth_sign(own - preds[d, 0, k].astype(F32))
        score = smooth_sign(own - target_cells[pl.ds(k * cells, cells), :])
        for d in range(1, chips):
            passed_on[k][d - 1].wait_recv()
            total += smooth_sign(own - preds[d, 1, k].astype(F32))
        pred_grad = score - total * (1.0 / (members - 1.0))
        turned = pred_grad.T.astype(BF16)
        part = jnp.dot(turned, act_buf[k], preferred_element_type=F32)
        part = part[:channels, :hidden] + part[channels:, hidden:]
        if k == 0:
            head_acc[...] = part
        else:
            head_acc[...] += part
        return pred_grad.astype(BF16)

    stores = []

    def backward_hidden(k, pred_grad):
        act_grad = jnp.dot(pred_grad, weight_pair[...], preferred_element_type=F32)
        grad = (act_grad * gate_buf[k]).astype(BF16)
        for side in range(2):
            hidden_buf[k, :, pl.ds(side * half, half), :] = grad[
                :, side * hidden : (side + 1) * hidden
            ].reshape(rows, half, hidden)
        copy = pltpu.make_async_copy(
            hidden_buf.at[k], hidden_grad.at[0, pl.ds(k * rows, rows)], out_sem.at[k]
        )
        copy.start()
        stores.append(copy)

    passed_on = []
    grads = []

    def receive(k):
        passed = []
        for d in range(1, chips):
            own_copies[k][d - 1].wait_recv()
            copy = member_copy(preds.at[d, 0, k], (d, 1), k, sibling)
            copy.start()
            passed.append(copy)
        passed_on.append(passed)

    receive(0)
    for k in range(CHUNKS):
        if k + 1 < CHUNKS:
            receive(k + 1)
        grads.append(backward_scores(k))
        if k < CHUNKS - TAIL:
            backward_hidden(k, grads[k])

    packed = grid_send.shape[1]
    scaled = head_acc[...] * (1.0 / (members * band_rows * columns * grid_count))
    blocks = jnp.concatenate([scaled, scaled], axis=0).T.reshape(grid_count, 2 * packed, LANES)
    lane = lax.broadcasted_iota(jnp.int32, (grid_count, packed, LANES), 2)
    grid_send[...] = jnp.where(
        lane < channels, blocks[:, :packed], blocks[:, packed:]
    ).astype(grid_send.dtype)
    grid_copies = []
    for offset in range(1, grid_count):
        peer = lax.rem(grid + offset, grid_count)
        copy = pltpu.make_async_remote_copy(
            src_ref=grid_send.at[peer],
            dst_ref=grid_recv.at[offset - 1],
            send_sem=grid_send_sem.at[offset - 1],
            recv_sem=grid_recv_sem.at[offset - 1],
            device_id={"grid": peer},
            device_id_type=pl.DeviceIdType.MESH,
        )
        copy.start()
        grid_copies.append(copy)
    for k in range(CHUNKS - TAIL, CHUNKS):
        backward_hidden(k, grads[k])

    total = grid_send[grid].astype(F32)
    for offset in range(1, grid_count):
        grid_copies[offset - 1].wait_recv()
        total += grid_recv[offset - 1].astype(F32)
    member_sum[member] = total

    def sum_copy(slot, offset):
        return pltpu.make_async_remote_copy(
            src_ref=member_sum.at[slot],
            dst_ref=member_sum.at[slot],
            send_sem=member_send_sem.at[offset - 1],
            recv_sem=member_recv_sem.at[offset - 1],
            device_id={"member": lax.rem(member + offset, members)},
            device_id_type=pl.DeviceIdType.MESH,
        )

    sum_copies = []
    for offset in range(1, members):
        copy = sum_copy(member, offset)
        copy.start()
        sum_copies.append(copy)

    for k in range(CHUNKS):
        sib_copies[k].wait_send()
        for copy in own_copies[k]:
            copy.wait_send()
        for copy in passed_on[k]:
            copy.wait_send()
    for copy in grid_copies:
        copy.wait_send()
    for copy in stores:
        copy.wait()
    for offset in range(1, members):
        sum_copy(lax.rem(member + members - offset, members), offset).wait_recv()
    head = member_sum[0]
    for other in range(1, members):
        head += member_sum[other]
    head_grad[...] = jnp.concatenate([head[:, :channels], head[:, channels:]], axis=0)
    for copy in sum_copies:
        copy.wait_send()


def local(features, perturbation, target, head_weight, head_bias):
    members = lax.axis_size("member")
    grid_count = lax.axis_size("grid")
    _, band_rows, columns, hidden = features.shape
    channels = head_weight.shape[1]
    half = columns // 2
    rows = band_rows // CHUNKS
    cells = rows * half
    chips = members // 2
    head_rows = hidden // grid_count
    packed = head_rows // 2
    sum_dtype = BF16 if packed % 16 == 0 else F32
    dma = pltpu.SemaphoreType.DMA
    vmem = pl.BlockSpec(memory_space=pltpu.VMEM)
    hbm = pl.BlockSpec(memory_space=pl.ANY)
    return pl.pallas_call(
        functools.partial(kernel, members, grid_count),
        out_shape=(
            jax.ShapeDtypeStruct(features.shape, BF16),
            jax.ShapeDtypeStruct((head_rows, channels), F32),
        ),
        in_specs=[hbm, hbm, hbm, vmem, vmem],
        out_specs=(hbm, vmem),
        scratch_shapes=[
            pltpu.VMEM((CHUNKS, rows, columns, hidden), BF16),
            pltpu.VMEM((CHUNKS, rows, columns, hidden), BF16),
            pltpu.VMEM(target.shape, BF16),
            pltpu.VMEM((band_rows * half, LANES), F32),
            pltpu.VMEM((2 * channels, 2 * hidden), BF16),
            pltpu.VMEM((CHUNKS, cells, 2 * hidden), BF16),
            pltpu.VMEM((CHUNKS, cells, 2 * hidden), F32),
            pltpu.VMEM((chips, 2, CHUNKS, cells, LANES), BF16),
            pltpu.VMEM((CHUNKS, rows, columns, hidden), BF16),
            pltpu.VMEM((channels, hidden), F32),
            pltpu.VMEM((grid_count, packed, LANES), sum_dtype),
            pltpu.VMEM((grid_count - 1, packed, LANES), sum_dtype),
            pltpu.VMEM((members, packed, LANES), F32),
            dma((2, CHUNKS)),
            dma,
            dma((CHUNKS,)),
            dma((chips, 2, CHUNKS)),
            dma((chips, 2, CHUNKS)),
            dma((grid_count - 1,)),
            dma((grid_count - 1,)),
            dma((members - 1,)),
            dma((members - 1,)),
        ],
        compiler_params=pltpu.CompilerParams(
            collective_id=0, has_side_effects=True, vmem_limit_bytes=48 * 1024 * 1024
        ),
        cost_estimate=pl.CostEstimate(
            flops=6 * band_rows * columns * hidden * channels,
            bytes_accessed=7 * band_rows * columns * hidden,
            transcendentals=2 * band_rows * columns * hidden,
        ),
    )(features, perturbation, target, head_weight.T, head_bias[None])


def solution(mesh):
    return jax.shard_map(
        local,
        mesh=mesh,
        in_specs=(
            P("member", None, "grid", None),
            P("member", None, "grid", None),
            P(None, "grid"),
            P(),
            P(),
        ),
        out_specs=(P("member", None, "grid", None), P("grid", None)),
        check_vma=False,
    )
```

```python
import functools

import jax
import jax.numpy as jnp
from jax import lax
from jax.experimental import pallas as pl
from jax.experimental.pallas import tpu as pltpu
from jax.sharding import PartitionSpec as P

F32 = jnp.float32
BF16 = jnp.bfloat16
LANES = 128
CHUNKS = 8
TAIL = 2
DIRECT = 1


def smooth_sign(value):
    return value * lax.rsqrt(value * value + 0.01)


def kernel(
    members,
    grid_count,
    features,
    perturbation,
    target,
    weight_hbm,
    bias_hbm,
    hidden_grad,
    head_grad,
    weight_t,
    bias,
    feat_buf,
    pert_buf,
    target_buf,
    target_cells,
    weight_pair,
    act_buf,
    sibling_act,
    gate_buf,
    preds,
    head_acc,
    sum_send,
    sum_recv,
    in_sem,
    small_sem,
    target_sem,
    pred_send_sem,
    pred_recv_sem,
    act_send_sem,
    act_recv_sem,
    sum_send_sem,
    sum_recv_sem,
):
    _, band_rows, columns, hidden = features.shape
    channels = weight_hbm.shape[0]
    half = columns // 2
    half_hidden = hidden // 2
    half_grid = grid_count // 2
    rows = band_rows // CHUNKS
    cells = rows * half
    chips = members // 2
    member = lax.axis_index("member")
    grid = lax.axis_index("grid")
    core = lax.rem(member, 2)
    chip = member // 2
    sibling = chip * 2 + 1 - core
    owner_core = grid // half_grid
    own_sum = core == owner_core
    mesh_ids = pl.DeviceIdType.MESH

    small_loads = []
    for which, (source, buffer) in enumerate(((weight_hbm, weight_t), (bias_hbm, bias))):
        copy = pltpu.make_async_copy(source, buffer, small_sem.at[which])
        copy.start()
        small_loads.append(copy)
    loads = []
    for k in range(CHUNKS):
        span = pl.ds(k * rows, rows)
        pair = []
        for which, (source, buffer) in enumerate(((features, feat_buf), (perturbation, pert_buf))):
            copy = pltpu.make_async_copy(source.at[0, span], buffer.at[k], in_sem.at[which, k])
            copy.start()
            pair.append(copy)
        loads.append(pair)
    target_load = pltpu.make_async_copy(target, target_buf, target_sem)
    target_load.start()

    barrier = pltpu.get_barrier_semaphore()

    def greet(device):
        pl.semaphore_signal(barrier, inc=1, device_id=device, device_id_type=mesh_ids)

    for offset in range(1, members):
        greet({"member": lax.rem(member + offset, members)})
    for q in range(chips):
        for i in range(grid_count):
            device = {
                "member": lax.rem(chip + q, chips) * 2 + owner_core,
                "grid": lax.rem(grid + i, grid_count),
            }
            if q == 0 and i == 0:
                pl.when(jnp.logical_not(own_sum))(functools.partial(greet, device))
            else:
                greet(device)

    for copy in small_loads:
        copy.wait()
    zero = jnp.zeros((channels, half_hidden), BF16)
    for part in range(2):
        lanes = pl.ds(part * half_hidden, half_hidden)
        weight_pair[part, :channels, :half_hidden] = weight_t[:, lanes]
        weight_pair[part, :channels, half_hidden:] = zero
        weight_pair[part, channels:, :half_hidden] = zero
        weight_pair[part, channels:, half_hidden:] = weight_t[:, lanes]
    bias_pair = jnp.concatenate([bias[...], bias[...]], axis=1)

    def member_copy(source, slot, k, device):
        return pltpu.make_async_remote_copy(
            src_ref=source,
            dst_ref=preds.at[slot[0], slot[1], k],
            send_sem=pred_send_sem.at[slot[0], slot[1], k],
            recv_sem=pred_recv_sem.at[slot[0], slot[1], k],
            device_id={"member": device},
            device_id_type=mesh_ids,
        )

    def forward(k):
        for copy in loads[k]:
            copy.wait()
        for side in range(2):
            cols = pl.ds(side * half, half)
            lanes = pl.ds(side * half_hidden, half_hidden)
            pre_act = feat_buf[k, :, cols, :].astype(F32) + pert_buf[k, :, cols, :].astype(F32)
            pre_act = pre_act.reshape(cells, hidden)
            gate = 0.5 + 0.5 * jnp.tanh(0.5 * pre_act)
            activated = pre_act * gate
            slope = gate + activated * (1.0 - gate)
            activated = activated.astype(BF16)
            for part in range(2):
                features_of = slice(part * half_hidden, (part + 1) * half_hidden)
                act_buf[part, k, :, lanes] = activated[:, features_of]
                gate_buf[part, k, :, lanes] = slope[:, features_of]
        pred = bias_pair
        for part in range(2):
            pred = pred + lax.dot_general(
                act_buf[part, k],
                weight_pair[part],
                (((1,), (1,)), ((), ())),
                preferred_element_type=F32,
            )
        preds[0, 0, k] = pred.astype(BF16)

    own_copies = []
    sib_copies = []
    act_copies = []
    passed_on = []
    for k in range(CHUNKS):
        forward(k)
        if k == 0:

            @pl.when(own_sum)
            def _():
                pl.semaphore_wait(barrier, members - 1 + members * half_grid - 1)

            @pl.when(jnp.logical_not(own_sum))
            def _():
                pl.semaphore_wait(barrier, members - 1 + members * half_grid)

        across = []
        beyond = []
        for d in range(1, chips):
            to_chip = lax.rem(chip + chips - d, chips)
            copy = member_copy(preds.at[0, 0, k], (d, 0), k, to_chip * 2 + core)
            copy.start()
            across.append(copy)
            if k >= CHUNKS - DIRECT:
                copy = member_copy(preds.at[0, 0, k], (d, 1), k, to_chip * 2 + 1 - core)
                copy.start()
                beyond.append(copy)
        own_copies.append(across)
        passed_on.append(beyond)
        copy = member_copy(preds.at[0, 0, k], (0, 1), k, sibling)
        copy.start()
        sib_copies.append(copy)
        copy = pltpu.make_async_remote_copy(
            src_ref=act_buf.at[1 - core, k],
            dst_ref=sibling_act.at[k],
            send_sem=act_send_sem.at[k],
            recv_sem=act_recv_sem.at[k],
            device_id={"member": sibling},
            device_id_type=mesh_ids,
        )
        copy.start()
        act_copies.append(copy)

    target_load.wait()
    low = lax.broadcasted_iota(jnp.int32, (band_rows, LANES), 1) < channels
    for i in range(half // 2):
        first = target_buf[:, pl.ds(i * LANES, LANES)].astype(F32)
        second = target_buf[:, pl.ds((half // 2 + i) * LANES, LANES)].astype(F32)
        even = jnp.where(low, first, pltpu.roll(second, channels, 1))
        odd = jnp.where(low, pltpu.roll(first, channels, 1), second)
        target_cells[pl.ds(2 * i, band_rows, stride=half), :] = even
        target_cells[pl.ds(2 * i + 1, band_rows, stride=half), :] = odd

    def receive(k):
        for d in range(1, chips):
            own_copies[k][d - 1].wait_recv()
            if k < CHUNKS - DIRECT:
                copy = member_copy(preds.at[d, 0, k], (d, 1), k, sibling)
                copy.start()
                passed_on[k].append(copy)

    pair_scale = 1.0 / (members - 1.0)

    def backward_scores(k):
        own = preds[0, 0, k].astype(F32)
        sib_copies[k].wait_recv()
        sib = preds[0, 1, k].astype(F32)
        observed = target_cells[pl.ds(k * cells, cells), :]
        own_total = smooth_sign(own - sib)
        sib_total = -own_total
        own_score = smooth_sign(own - observed)
        sib_score = smooth_sign(sib - observed)
        for d in range(1, chips):
            passed_on[k][d - 1].wait_recv()
            for other_core in range(2):
                other = preds[d, other_core, k].astype(F32)
                own_total += smooth_sign(own - other)
                sib_total += smooth_sign(sib - other)
        own_grad = own_score - own_total * pair_scale
        sib_grad = sib_score - sib_total * pair_scale
        act_copies[k].wait_recv()
        part = jnp.dot(
            own_grad.T.astype(BF16), act_buf[core, k], preferred_element_type=F32
        ) + jnp.dot(sib_grad.T.astype(BF16), sibling_act[k], preferred_element_type=F32)
        part = part[:channels, :half_hidden] + part[channels:, half_hidden:]
        if k == 0:
            head_acc[...] = part
        else:
            head_acc[...] += part
        return own_grad.astype(BF16)

    def backward_hidden(k, pred_grad):
        for part in range(2):
            act_grad = jnp.dot(pred_grad, weight_pair[part], preferred_element_type=F32)
            grad = (act_grad * gate_buf[part, k]).astype(BF16)
            for side in range(2):
                hidden_grad[
                    0,
                    pl.ds(k * rows, rows),
                    pl.ds(side * half, half),
                    pl.ds(part * half_hidden, half_hidden),
                ] = grad[:, side * half_hidden : (side + 1) * half_hidden].reshape(
                    rows, half, half_hidden
                )

    grads = []
    receive(0)
    for k in range(CHUNKS):
        if k + 1 < CHUNKS:
            receive(k + 1)
        grads.append(backward_scores(k))
        if k < CHUNKS - TAIL:
            backward_hidden(k, grads[k])

    packed = sum_send.shape[1]
    scaled = head_acc[...] * (1.0 / (members * band_rows * columns * grid_count))
    blocks = jnp.concatenate([scaled, scaled], axis=0).T.reshape(half_grid, 2 * packed, LANES)
    lane = lax.broadcasted_iota(jnp.int32, (half_grid, packed, LANES), 2)
    sum_send[...] = jnp.where(
        lane < channels, blocks[:, :packed], blocks[:, packed:]
    ).astype(sum_send.dtype)

    def sum_copy(o, b):
        block = lax.rem(grid + b, half_grid)
        return pltpu.make_async_remote_copy(
            src_ref=sum_send.at[block],
            dst_ref=sum_recv.at[chip, grid],
            send_sem=sum_send_sem.at[o, b],
            recv_sem=sum_recv_sem.at[chip, grid],
            device_id={
                "member": lax.rem(member + o, members),
                "grid": core * half_grid + block,
            },
            device_id_type=mesh_ids,
        )

    for b in reversed(range(half_grid)):
        for o in reversed(range(members)):
            if o == 0 and b == 0:

                @pl.when(jnp.logical_not(own_sum))
                def _():
                    sum_copy(0, 0).start()

                @pl.when(own_sum)
                def _():
                    sum_recv[chip, grid] = sum_send[lax.rem(grid, half_grid)]

            else:
                sum_copy(o, b).start()

    for k in range(CHUNKS - TAIL, CHUNKS):
        backward_hidden(k, grads[k])

    for k in range(CHUNKS):
        sib_copies[k].wait_send()
        act_copies[k].wait_send()
        for copy in own_copies[k]:
            copy.wait_send()
        for copy in passed_on[k]:
            copy.wait_send()

    def arrived(source_chip, source_grid):
        pltpu.make_async_remote_copy(
            src_ref=sum_send.at[0],
            dst_ref=sum_recv.at[source_chip, source_grid],
            send_sem=sum_send_sem.at[0, 0],
            recv_sem=sum_recv_sem.at[source_chip, source_grid],
            device_id={"member": sibling},
            device_id_type=mesh_ids,
        ).wait_recv()

    for q in range(chips):
        for i in range(grid_count):
            wait = functools.partial(
                arrived, lax.rem(chip + q, chips), lax.rem(grid + i, grid_count)
            )
            if q == 0 and i == 0:
                pl.when(jnp.logical_not(own_sum))(wait)
            else:
                wait()
    head = jnp.sum(
        sum_recv[...].astype(F32).reshape(chips * grid_count, packed, LANES), axis=0
    )
    head_grad[...] = jnp.concatenate([head[:, :channels], head[:, channels:]], axis=0)
    for o in range(members):
        for b in range(half_grid):
            if o == 0 and b == 0:

                @pl.when(jnp.logical_not(own_sum))
                def _():
                    sum_copy(0, 0).wait_send()

            else:
                sum_copy(o, b).wait_send()


def local(features, perturbation, target, head_weight, head_bias):
    members = lax.axis_size("member")
    grid_count = lax.axis_size("grid")
    _, band_rows, columns, hidden = features.shape
    channels = head_weight.shape[1]
    half = columns // 2
    rows = band_rows // CHUNKS
    cells = rows * half
    chips = members // 2
    head_rows = hidden // grid_count
    packed = head_rows // 2
    sum_dtype = BF16 if packed % 16 == 0 else F32
    dma = pltpu.SemaphoreType.DMA
    vmem = pl.BlockSpec(memory_space=pltpu.VMEM)
    hbm = pl.BlockSpec(memory_space=pl.ANY)
    return pl.pallas_call(
        functools.partial(kernel, members, grid_count),
        out_shape=(
            pltpu.VMEM(features.shape, BF16),
            jax.ShapeDtypeStruct((head_rows, channels), F32),
        ),
        in_specs=[hbm, hbm, hbm, hbm, hbm],
        out_specs=(vmem, vmem),
        scratch_shapes=[
            pltpu.VMEM((channels, hidden), BF16),
            pltpu.VMEM((1, channels), F32),
            pltpu.VMEM((CHUNKS, rows, columns, hidden), BF16),
            pltpu.VMEM((CHUNKS, rows, columns, hidden), BF16),
            pltpu.VMEM(target.shape, BF16),
            pltpu.VMEM((band_rows * half, LANES), F32),
            pltpu.VMEM((2, 2 * channels, hidden), BF16),
            pltpu.VMEM((2, CHUNKS, cells, hidden), BF16),
            pltpu.VMEM((CHUNKS, cells, hidden), BF16),
            pltpu.VMEM((2, CHUNKS, cells, hidden), F32),
            pltpu.VMEM((chips, 2, CHUNKS, cells, LANES), BF16),
            pltpu.VMEM((channels, hidden // 2), F32),
            pltpu.VMEM((grid_count // 2, packed, LANES), sum_dtype),
            pltpu.VMEM((chips, grid_count, packed, LANES), sum_dtype),
            dma((2, CHUNKS)),
            dma((2,)),
            dma,
            dma((chips, 2, CHUNKS)),
            dma((chips, 2, CHUNKS)),
            dma((CHUNKS,)),
            dma((CHUNKS,)),
            dma((members, grid_count // 2)),
            dma((chips, grid_count)),
        ],
        compiler_params=pltpu.CompilerParams(
            collective_id=0, has_side_effects=True, vmem_limit_bytes=56 * 1024 * 1024
        ),
        cost_estimate=pl.CostEstimate(
            flops=6 * band_rows * columns * hidden * channels,
            bytes_accessed=7 * band_rows * columns * hidden,
            transcendentals=2 * band_rows * columns * hidden,
        ),
    )(features, perturbation, target, head_weight.T, head_bias[None])


def solution(mesh):
    return jax.shard_map(
        local,
        mesh=mesh,
        in_specs=(
            P("member", None, "grid", None),
            P("member", None, "grid", None),
            P(None, "grid"),
            P(),
            P(),
        ),
        out_specs=(P("member", None, "grid", None), P("grid", None)),
        check_vma=False,
    )
```

```python
import functools

import jax
import jax.numpy as jnp
from jax import lax
from jax.experimental import pallas as pl
from jax.experimental.pallas import tpu as pltpu
from jax.sharding import PartitionSpec as P

F32 = jnp.float32
BF16 = jnp.bfloat16
LANES = 128
EIGHTHS = (1, 2, 2, 2, 1)
CHUNKS = len(EIGHTHS)
TAIL = 2
DIRECT = 1


def smooth_sign(value):
    return value * lax.rsqrt(value * value + 0.01)


def kernel(
    members,
    grid_count,
    features,
    perturbation,
    target,
    weight_hbm,
    bias_hbm,
    hidden_grad,
    head_grad,
    weight_t,
    bias,
    feat_buf,
    pert_buf,
    target_buf,
    target_cells,
    weight_pair,
    weight_turned,
    act_buf,
    sibling_act,
    gate_buf,
    preds,
    head_acc,
    sum_send,
    sum_recv,
    in_sem,
    small_sem,
    target_sem,
    pred_send_sem,
    pred_recv_sem,
    act_send_sem,
    act_recv_sem,
    sum_send_sem,
    sum_recv_sem,
):
    _, band_rows, columns, hidden = features.shape
    channels = weight_hbm.shape[0]
    half = columns // 2
    half_hidden = hidden // 2
    half_grid = grid_count // 2
    starts = [sum(EIGHTHS[:k]) * band_rows // 8 for k in range(CHUNKS + 1)]
    chips = members // 2
    member = lax.axis_index("member")
    grid = lax.axis_index("grid")
    core = lax.rem(member, 2)
    chip = member // 2
    sibling = chip * 2 + 1 - core
    owner_core = grid // half_grid
    own_sum = core == owner_core
    mesh_ids = pl.DeviceIdType.MESH

    def row_span(k):
        return pl.ds(starts[k], starts[k + 1] - starts[k])

    def cell_span(k):
        return pl.ds(starts[k] * half, (starts[k + 1] - starts[k]) * half)

    small_loads = []
    for which, (source, buffer) in enumerate(((weight_hbm, weight_t), (bias_hbm, bias))):
        copy = pltpu.make_async_copy(source, buffer, small_sem.at[which])
        copy.start()
        small_loads.append(copy)
    loads = []
    for k in range(CHUNKS):
        pair = []
        for which, (source, buffer) in enumerate(((features, feat_buf), (perturbation, pert_buf))):
            copy = pltpu.make_async_copy(
                source.at[0, row_span(k)], buffer.at[row_span(k)], in_sem.at[which, k]
            )
            pair.append(copy)
        loads.append(pair)
    target_load = pltpu.make_async_copy(target, target_buf, target_sem)
    for copy in loads[0]:
        copy.start()

    barrier = pltpu.get_barrier_semaphore()

    def greet(device):
        pl.semaphore_signal(barrier, inc=1, device_id=device, device_id_type=mesh_ids)

    for offset in range(1, members):
        greet({"member": lax.rem(member + offset, members)})
    for q in range(chips):
        for i in range(grid_count):
            device = {
                "member": lax.rem(chip + q, chips) * 2 + owner_core,
                "grid": lax.rem(grid + i, grid_count),
            }
            if q == 0 and i == 0:
                pl.when(jnp.logical_not(own_sum))(functools.partial(greet, device))
            else:
                greet(device)

    for pair in loads[1:]:
        for copy in pair:
            copy.start()
    target_load.start()
    for copy in small_loads:
        copy.wait()
    zero = jnp.zeros((channels, half_hidden), BF16)
    for part in range(2):
        lanes = pl.ds(part * half_hidden, half_hidden)
        weight_pair[part, :channels, :half_hidden] = weight_t[:, lanes]
        weight_pair[part, :channels, half_hidden:] = zero
        weight_pair[part, channels:, :half_hidden] = zero
        weight_pair[part, channels:, half_hidden:] = weight_t[:, lanes]
        weight_turned[part] = weight_pair[part].T
    bias_pair = jnp.concatenate([bias[...], bias[...]], axis=1)

    def member_copy(source, slot, k, device):
        return pltpu.make_async_remote_copy(
            src_ref=source,
            dst_ref=preds.at[slot[0], slot[1], cell_span(k)],
            send_sem=pred_send_sem.at[slot[0], slot[1], k],
            recv_sem=pred_recv_sem.at[slot[0], slot[1], k],
            device_id={"member": device},
            device_id_type=mesh_ids,
        )

    def forward(k):
        for copy in loads[k]:
            copy.wait()
        for side in range(2):
            cols = pl.ds(side * half, half)
            lanes = pl.ds(side * half_hidden, half_hidden)
            pre_act = feat_buf[row_span(k), cols, :].astype(F32) + pert_buf[row_span(k), cols, :].astype(F32)
            pre_act = pre_act.reshape(-1, hidden)
            gate = 0.5 + 0.5 * jnp.tanh(0.5 * pre_act)
            activated = pre_act * gate
            slope = gate + activated * (1.0 - gate)
            activated = activated.astype(BF16)
            for part in range(2):
                features_of = slice(part * half_hidden, (part + 1) * half_hidden)
                act_buf[part, cell_span(k), lanes] = activated[:, features_of]
                gate_buf[part, cell_span(k), lanes] = slope[:, features_of]
        pred = bias_pair
        for part in range(2):
            pred = pred + lax.dot_general(
                act_buf[part, cell_span(k), :],
                weight_turned[part],
                (((1,), (0,)), ((), ())),
                preferred_element_type=F32,
            )
        preds[0, 0, cell_span(k), :] = pred.astype(BF16)

    own_copies = []
    sib_copies = []
    act_copies = []
    passed_on = []
    for k in range(CHUNKS):
        forward(k)
        if k == 0:

            @pl.when(own_sum)
            def _():
                pl.semaphore_wait(barrier, members - 1 + members * half_grid - 1)

            @pl.when(jnp.logical_not(own_sum))
            def _():
                pl.semaphore_wait(barrier, members - 1 + members * half_grid)

        across = []
        beyond = []
        for d in range(1, chips):
            to_chip = lax.rem(chip + chips - d, chips)
            copy = member_copy(preds.at[0, 0, cell_span(k)], (d, 0), k, to_chip * 2 + core)
            copy.start()
            across.append(copy)
            if k >= CHUNKS - DIRECT:
                copy = member_copy(preds.at[0, 0, cell_span(k)], (d, 1), k, to_chip * 2 + 1 - core)
                copy.start()
                beyond.append(copy)
        own_copies.append(across)
        passed_on.append(beyond)
        copy = member_copy(preds.at[0, 0, cell_span(k)], (0, 1), k, sibling)
        copy.start()
        sib_copies.append(copy)
        copy = pltpu.make_async_remote_copy(
            src_ref=act_buf.at[1 - core, cell_span(k)],
            dst_ref=sibling_act.at[cell_span(k)],
            send_sem=act_send_sem.at[k],
            recv_sem=act_recv_sem.at[k],
            device_id={"member": sibling},
            device_id_type=mesh_ids,
        )
        copy.start()
        act_copies.append(copy)

    target_load.wait()
    low = lax.broadcasted_iota(jnp.int32, (band_rows, LANES), 1) < channels
    for i in range(half // 2):
        first = target_buf[:, pl.ds(i * LANES, LANES)].astype(F32)
        second = target_buf[:, pl.ds((half // 2 + i) * LANES, LANES)].astype(F32)
        even = jnp.where(low, first, pltpu.roll(second, channels, 1))
        odd = jnp.where(low, pltpu.roll(first, channels, 1), second)
        target_cells[pl.ds(2 * i, band_rows, stride=half), :] = even
        target_cells[pl.ds(2 * i + 1, band_rows, stride=half), :] = odd

    def receive(k):
        if k < CHUNKS - DIRECT:
            for d in range(1, chips):
                own_copies[k][d - 1].wait_recv()
                copy = member_copy(preds.at[d, 0, cell_span(k)], (d, 1), k, sibling)
                copy.start()
                passed_on[k].append(copy)

    pair_scale = 1.0 / (members - 1.0)

    def backward_scores(k):
        own = preds[0, 0, cell_span(k), :].astype(F32)
        sib_copies[k].wait_recv()
        sib = preds[0, 1, cell_span(k), :].astype(F32)
        observed = target_cells[cell_span(k), :]
        own_total = smooth_sign(own - sib)
        sib_total = -own_total
        own_score = smooth_sign(own - observed)
        sib_score = smooth_sign(sib - observed)
        for d in range(1, chips):
            if k >= CHUNKS - DIRECT:
                own_copies[k][d - 1].wait_recv()
            passed_on[k][d - 1].wait_recv()
            for other_core in range(2):
                other = preds[d, other_core, cell_span(k), :].astype(F32)
                own_total += smooth_sign(own - other)
                sib_total += smooth_sign(sib - other)
        own_grad = own_score - own_total * pair_scale
        sib_grad = sib_score - sib_total * pair_scale
        act_copies[k].wait_recv()
        part = jnp.dot(
            own_grad.T.astype(BF16), act_buf[core, cell_span(k), :], preferred_element_type=F32
        ) + jnp.dot(sib_grad.T.astype(BF16), sibling_act[cell_span(k), :], preferred_element_type=F32)
        part = part[:channels, :half_hidden] + part[channels:, half_hidden:]
        if k == 0:
            head_acc[...] = part
        else:
            head_acc[...] += part
        return own_grad.astype(BF16)

    def backward_hidden(k, pred_grad):
        for part in range(2):
            act_grad = jnp.dot(pred_grad, weight_pair[part], preferred_element_type=F32)
            grad = (act_grad * gate_buf[part, cell_span(k), :]).astype(BF16)
            for side in range(2):
                hidden_grad[
                    0,
                    row_span(k),
                    pl.ds(side * half, half),
                    pl.ds(part * half_hidden, half_hidden),
                ] = grad[:, side * half_hidden : (side + 1) * half_hidden].reshape(
                    -1, half, half_hidden
                )

    grads = []
    receive(0)
    for k in range(CHUNKS):
        if k + 1 < CHUNKS:
            receive(k + 1)
        grads.append(backward_scores(k))
        if k < CHUNKS - TAIL:
            backward_hidden(k, grads[k])

    packed = sum_send.shape[1]
    scaled = head_acc[...] * (1.0 / (members * band_rows * columns * grid_count))
    blocks = jnp.concatenate([scaled, scaled], axis=0).T.reshape(half_grid, 2 * packed, LANES)
    lane = lax.broadcasted_iota(jnp.int32, (half_grid, packed, LANES), 2)
    sum_send[...] = jnp.where(
        lane < channels, blocks[:, :packed], blocks[:, packed:]
    ).astype(sum_send.dtype)

    def sum_copy(o, b):
        block = lax.rem(grid + b, half_grid)
        return pltpu.make_async_remote_copy(
            src_ref=sum_send.at[block],
            dst_ref=sum_recv.at[chip, grid],
            send_sem=sum_send_sem.at[o, b],
            recv_sem=sum_recv_sem.at[chip, grid],
            device_id={
                "member": lax.rem(member + o, members),
                "grid": core * half_grid + block,
            },
            device_id_type=mesh_ids,
        )

    for b in range(half_grid):
        for o in range(members):
            if o == 0 and b == 0:

                @pl.when(jnp.logical_not(own_sum))
                def _():
                    sum_copy(0, 0).start()

                @pl.when(own_sum)
                def _():
                    sum_recv[chip, grid] = sum_send[lax.rem(grid, half_grid)]

            else:
                sum_copy(o, b).start()

    for k in range(CHUNKS - TAIL, CHUNKS):
        backward_hidden(k, grads[k])

    for k in range(CHUNKS):
        sib_copies[k].wait_send()
        act_copies[k].wait_send()
        for copy in own_copies[k]:
            copy.wait_send()
        for copy in passed_on[k]:
            copy.wait_send()

    def arrived(source_chip, source_grid):
        pltpu.make_async_remote_copy(
            src_ref=sum_send.at[0],
            dst_ref=sum_recv.at[source_chip, source_grid],
            send_sem=sum_send_sem.at[0, 0],
            recv_sem=sum_recv_sem.at[source_chip, source_grid],
            device_id={"member": sibling},
            device_id_type=mesh_ids,
        ).wait_recv()

    for q in range(chips):
        for i in range(grid_count):
            wait = functools.partial(
                arrived, lax.rem(chip + q, chips), lax.rem(grid + i, grid_count)
            )
            if q == 0 and i == 0:
                pl.when(jnp.logical_not(own_sum))(wait)
            else:
                wait()
    head = jnp.sum(
        sum_recv[...].astype(F32).reshape(chips * grid_count, packed, LANES), axis=0
    )
    head_grad[...] = jnp.concatenate([head[:, :channels], head[:, channels:]], axis=0)
    for o in range(members):
        for b in range(half_grid):
            if o == 0 and b == 0:

                @pl.when(jnp.logical_not(own_sum))
                def _():
                    sum_copy(0, 0).wait_send()

            else:
                sum_copy(o, b).wait_send()


def local(features, perturbation, target, head_weight, head_bias):
    members = lax.axis_size("member")
    grid_count = lax.axis_size("grid")
    _, band_rows, columns, hidden = features.shape
    channels = head_weight.shape[1]
    half = columns // 2
    cells = band_rows * half
    chips = members // 2
    head_rows = hidden // grid_count
    packed = head_rows // 2
    sum_dtype = BF16 if packed % 16 == 0 else F32
    dma = pltpu.SemaphoreType.DMA
    vmem = pl.BlockSpec(memory_space=pltpu.VMEM)
    hbm = pl.BlockSpec(memory_space=pl.ANY)
    return pl.pallas_call(
        functools.partial(kernel, members, grid_count),
        out_shape=(
            pltpu.VMEM(features.shape, BF16),
            jax.ShapeDtypeStruct((head_rows, channels), F32),
        ),
        in_specs=[hbm, hbm, hbm, hbm, hbm],
        out_specs=(vmem, vmem),
        scratch_shapes=[
            pltpu.VMEM((channels, hidden), BF16),
            pltpu.VMEM((1, channels), F32),
            pltpu.VMEM((band_rows, columns, hidden), BF16),
            pltpu.VMEM((band_rows, columns, hidden), BF16),
            pltpu.VMEM(target.shape, BF16),
            pltpu.VMEM((band_rows * half, LANES), F32),
            pltpu.VMEM((2, 2 * channels, hidden), BF16),
            pltpu.VMEM((2, hidden, 2 * channels), BF16),
            pltpu.VMEM((2, cells, hidden), BF16),
            pltpu.VMEM((cells, hidden), BF16),
            pltpu.VMEM((2, cells, hidden), F32),
            pltpu.VMEM((chips, 2, cells, LANES), BF16),
            pltpu.VMEM((channels, hidden // 2), F32),
            pltpu.VMEM((grid_count // 2, packed, LANES), sum_dtype),
            pltpu.VMEM((chips, grid_count, packed, LANES), sum_dtype),
            dma((2, CHUNKS)),
            dma((2,)),
            dma,
            dma((chips, 2, CHUNKS)),
            dma((chips, 2, CHUNKS)),
            dma((CHUNKS,)),
            dma((CHUNKS,)),
            dma((members, grid_count // 2)),
            dma((chips, grid_count)),
        ],
        compiler_params=pltpu.CompilerParams(
            collective_id=0, has_side_effects=True, vmem_limit_bytes=56 * 1024 * 1024
        ),
        cost_estimate=pl.CostEstimate(
            flops=6 * band_rows * columns * hidden * channels,
            bytes_accessed=7 * band_rows * columns * hidden,
            transcendentals=2 * band_rows * columns * hidden,
        ),
    )(features, perturbation, target, head_weight.T, head_bias[None])


def solution(mesh):
    return jax.shard_map(
        local,
        mesh=mesh,
        in_specs=(
            P("member", None, "grid", None),
            P("member", None, "grid", None),
            P(None, "grid"),
            P(),
            P(),
        ),
        out_specs=(P("member", None, "grid", None), P("grid", None)),
        check_vma=False,
    )
```

```python
import functools

import jax
import jax.numpy as jnp
from jax import lax
from jax.experimental import pallas as pl
from jax.experimental.pallas import tpu as pltpu
from jax.sharding import PartitionSpec as P

F32 = jnp.float32
BF16 = jnp.bfloat16
LANES = 128
EIGHTHS = (1, 2, 2, 2, 1)
CHUNKS = len(EIGHTHS)
TAIL = 2
DIRECT = 1


def smooth_sign(value):
    return value * lax.rsqrt(value * value + 0.01)


def kernel(
    members,
    grid_count,
    features,
    perturbation,
    target,
    weight_hbm,
    bias_hbm,
    hidden_grad,
    head_grad,
    weight_t,
    bias,
    feat_buf,
    pert_buf,
    target_buf,
    target_cells,
    weight_pair,
    weight_turned,
    act_buf,
    sibling_act,
    gate_buf,
    preds,
    head_acc,
    sum_send,
    sum_recv,
    in_sem,
    small_sem,
    target_sem,
    pred_send_sem,
    pred_recv_sem,
    act_send_sem,
    act_recv_sem,
    sum_send_sem,
    sum_recv_sem,
):
    _, band_rows, columns, hidden = features.shape
    channels = weight_hbm.shape[0]
    half = columns // 2
    half_hidden = hidden // 2
    half_grid = grid_count // 2
    starts = [sum(EIGHTHS[:k]) * band_rows // 8 for k in range(CHUNKS + 1)]
    chips = members // 2
    member = lax.axis_index("member")
    grid = lax.axis_index("grid")
    core = lax.rem(member, 2)
    chip = member // 2
    sibling = chip * 2 + 1 - core
    owner_core = grid // half_grid
    own_sum = core == owner_core
    mesh_ids = pl.DeviceIdType.MESH

    def row_span(k):
        return pl.ds(starts[k], starts[k + 1] - starts[k])

    def cell_span(k):
        return pl.ds(starts[k] * half, (starts[k + 1] - starts[k]) * half)

    small_loads = []
    for which, (source, buffer) in enumerate(((weight_hbm, weight_t), (bias_hbm, bias))):
        copy = pltpu.make_async_copy(source, buffer, small_sem.at[which])
        copy.start()
        small_loads.append(copy)
    loads = []
    for k in range(CHUNKS):
        pair = []
        for which, (source, buffer) in enumerate(((features, feat_buf), (perturbation, pert_buf))):
            copy = pltpu.make_async_copy(
                source.at[0, row_span(k)], buffer.at[row_span(k)], in_sem.at[which, k]
            )
            pair.append(copy)
        loads.append(pair)
    target_load = pltpu.make_async_copy(target, target_buf, target_sem)
    for copy in loads[0]:
        copy.start()

    barrier = pltpu.get_barrier_semaphore()

    def greet(device):
        pl.semaphore_signal(barrier, inc=1, device_id=device, device_id_type=mesh_ids)

    for offset in range(1, members):
        greet({"member": lax.rem(member + offset, members)})
    for q in range(chips):
        for i in range(grid_count):
            device = {
                "member": lax.rem(chip + q, chips) * 2 + owner_core,
                "grid": lax.rem(grid + i, grid_count),
            }
            if q == 0 and i == 0:
                pl.when(jnp.logical_not(own_sum))(functools.partial(greet, device))
            else:
                greet(device)

    for pair in loads[1:]:
        for copy in pair:
            copy.start()
    target_load.start()
    for copy in small_loads:
        copy.wait()
    zero = jnp.zeros((channels, half_hidden), BF16)
    for part in range(2):
        lanes = pl.ds(part * half_hidden, half_hidden)
        weight_pair[part, :channels, :half_hidden] = weight_t[:, lanes]
        weight_pair[part, :channels, half_hidden:] = zero
        weight_pair[part, channels:, :half_hidden] = zero
        weight_pair[part, channels:, half_hidden:] = weight_t[:, lanes]
        weight_turned[part] = weight_pair[part].T
    bias_pair = jnp.concatenate([bias[...], bias[...]], axis=1)

    def member_copy(source, slot, k, device):
        return pltpu.make_async_remote_copy(
            src_ref=source,
            dst_ref=preds.at[slot[0], slot[1], cell_span(k)],
            send_sem=pred_send_sem.at[slot[0], slot[1], k],
            recv_sem=pred_recv_sem.at[slot[0], slot[1], k],
            device_id={"member": device},
            device_id_type=mesh_ids,
        )

    def forward(k):
        for copy in loads[k]:
            copy.wait()
        for side in range(2):
            cols = pl.ds(side * half, half)
            lanes = pl.ds(side * half_hidden, half_hidden)
            pre_act = feat_buf[row_span(k), cols, :].astype(F32) + pert_buf[row_span(k), cols, :].astype(F32)
            pre_act = pre_act.reshape(-1, hidden)
            gate = 0.5 + 0.5 * jnp.tanh(0.5 * pre_act)
            activated = pre_act * gate
            slope = gate + activated * (1.0 - gate)
            activated = activated.astype(BF16)
            for part in range(2):
                features_of = slice(part * half_hidden, (part + 1) * half_hidden)
                act_buf[part, cell_span(k), lanes] = activated[:, features_of]
                gate_buf[part, cell_span(k), lanes] = slope[:, features_of]
        pred = bias_pair
        for part in range(2):
            pred = pred + lax.dot_general(
                act_buf[part, cell_span(k), :],
                weight_turned[part],
                (((1,), (0,)), ((), ())),
                preferred_element_type=F32,
            )
        preds[0, 0, cell_span(k), :] = pred.astype(BF16)

    own_copies = []
    sib_copies = []
    act_copies = []
    passed_on = []
    for k in range(CHUNKS):
        forward(k)
        if k == 0:

            @pl.when(own_sum)
            def _():
                pl.semaphore_wait(barrier, members - 1 + members * half_grid - 1)

            @pl.when(jnp.logical_not(own_sum))
            def _():
                pl.semaphore_wait(barrier, members - 1 + members * half_grid)

        across = []
        beyond = []
        for d in range(1, chips):
            to_chip = lax.rem(chip + chips - d, chips)
            copy = member_copy(preds.at[0, 0, cell_span(k)], (d, 0), k, to_chip * 2 + core)
            copy.start()
            across.append(copy)
            if k >= CHUNKS - DIRECT:
                copy = member_copy(preds.at[0, 0, cell_span(k)], (d, 1), k, to_chip * 2 + 1 - core)
                copy.start()
                beyond.append(copy)
        own_copies.append(across)
        passed_on.append(beyond)
        copy = member_copy(preds.at[0, 0, cell_span(k)], (0, 1), k, sibling)
        copy.start()
        sib_copies.append(copy)
        copy = pltpu.make_async_remote_copy(
            src_ref=act_buf.at[1 - core, cell_span(k)],
            dst_ref=sibling_act.at[cell_span(k)],
            send_sem=act_send_sem.at[k],
            recv_sem=act_recv_sem.at[k],
            device_id={"member": sibling},
            device_id_type=mesh_ids,
        )
        copy.start()
        act_copies.append(copy)

    target_load.wait()
    low = lax.broadcasted_iota(jnp.int32, (band_rows, LANES), 1) < channels
    for i in range(half // 2):
        first = target_buf[:, pl.ds(i * LANES, LANES)].astype(F32)
        second = target_buf[:, pl.ds((half // 2 + i) * LANES, LANES)].astype(F32)
        even = jnp.where(low, first, pltpu.roll(second, channels, 1))
        odd = jnp.where(low, pltpu.roll(first, channels, 1), second)
        target_cells[pl.ds(2 * i, band_rows, stride=half), :] = even
        target_cells[pl.ds(2 * i + 1, band_rows, stride=half), :] = odd

    def receive(k):
        if k < CHUNKS - DIRECT:
            for d in range(1, chips):
                own_copies[k][d - 1].wait_recv()
                copy = member_copy(preds.at[d, 0, cell_span(k)], (d, 1), k, sibling)
                copy.start()
                passed_on[k].append(copy)

    pair_scale = 1.0 / (members - 1.0)

    def backward_scores(k):
        own = preds[0, 0, cell_span(k), :].astype(F32)
        sib_copies[k].wait_recv()
        sib = preds[0, 1, cell_span(k), :].astype(F32)
        observed = target_cells[cell_span(k), :]
        own_total = smooth_sign(own - sib)
        sib_total = -own_total
        own_score = smooth_sign(own - observed)
        sib_score = smooth_sign(sib - observed)
        for d in range(1, chips):
            if k >= CHUNKS - DIRECT:
                own_copies[k][d - 1].wait_recv()
            passed_on[k][d - 1].wait_recv()
            for other_core in range(2):
                other = preds[d, other_core, cell_span(k), :].astype(F32)
                own_total += smooth_sign(own - other)
                sib_total += smooth_sign(sib - other)
        own_grad = own_score - own_total * pair_scale
        sib_grad = sib_score - sib_total * pair_scale
        act_copies[k].wait_recv()
        part = jnp.dot(
            own_grad.T.astype(BF16), act_buf[core, cell_span(k), :], preferred_element_type=F32
        ) + jnp.dot(sib_grad.T.astype(BF16), sibling_act[cell_span(k), :], preferred_element_type=F32)
        part = part[:channels, :half_hidden] + part[channels:, half_hidden:]
        if k == 0:
            head_acc[...] = part
        else:
            head_acc[...] += part
        return own_grad.astype(BF16)

    def backward_hidden(k, pred_grad):
        for part in range(2):
            act_grad = jnp.dot(pred_grad, weight_pair[part], preferred_element_type=F32)
            grad = (act_grad * gate_buf[part, cell_span(k), :]).astype(BF16)
            for side in range(2):
                hidden_grad[
                    0,
                    row_span(k),
                    pl.ds(side * half, half),
                    pl.ds(part * half_hidden, half_hidden),
                ] = grad[:, side * half_hidden : (side + 1) * half_hidden].reshape(
                    -1, half, half_hidden
                )

    grads = []
    receive(0)
    for k in range(CHUNKS):
        if k + 1 < CHUNKS:
            receive(k + 1)
        grads.append(backward_scores(k))
        if k < CHUNKS - TAIL:
            backward_hidden(k, grads[k])

    packed = sum_send.shape[1]
    scaled = head_acc[...] * (1.0 / (members * band_rows * columns * grid_count))
    blocks = jnp.concatenate([scaled, scaled], axis=0).T.reshape(half_grid, 2 * packed, LANES)
    lane = lax.broadcasted_iota(jnp.int32, (half_grid, packed, LANES), 2)
    sum_send[...] = jnp.where(
        lane < channels, blocks[:, :packed], blocks[:, packed:]
    ).astype(sum_send.dtype)

    def sum_copy(o, b):
        block = lax.rem(grid + b, half_grid)
        return pltpu.make_async_remote_copy(
            src_ref=sum_send.at[block],
            dst_ref=sum_recv.at[chip, grid],
            send_sem=sum_send_sem.at[o, b],
            recv_sem=sum_recv_sem.at[chip, grid],
            device_id={
                "member": lax.rem(member + o, members),
                "grid": core * half_grid + block,
            },
            device_id_type=mesh_ids,
        )

    for b in range(half_grid):
        for o in range(members):
            if o == 0 and b == 0:

                @pl.when(jnp.logical_not(own_sum))
                def _():
                    sum_copy(0, 0).start()

                @pl.when(own_sum)
                def _():
                    sum_recv[chip, grid] = sum_send[lax.rem(grid, half_grid)]

            else:
                sum_copy(o, b).start()

    for k in range(CHUNKS - TAIL, CHUNKS):
        backward_hidden(k, grads[k])

    for k in range(CHUNKS):
        sib_copies[k].wait_send()
        act_copies[k].wait_send()
        for copy in own_copies[k]:
            copy.wait_send()
        for copy in passed_on[k]:
            copy.wait_send()

    def arrived(source_chip, source_grid):
        pltpu.make_async_remote_copy(
            src_ref=sum_send.at[0],
            dst_ref=sum_recv.at[source_chip, source_grid],
            send_sem=sum_send_sem.at[0, 0],
            recv_sem=sum_recv_sem.at[source_chip, source_grid],
            device_id={"member": sibling},
            device_id_type=mesh_ids,
        ).wait_recv()

    for q in range(chips):
        for i in range(grid_count):
            wait = functools.partial(
                arrived, lax.rem(chip + q, chips), lax.rem(grid + i, grid_count)
            )
            if q == 0 and i == 0:
                pl.when(jnp.logical_not(own_sum))(wait)
            else:
                wait()
    head = jnp.sum(
        sum_recv[...].astype(F32).reshape(chips * grid_count, packed, LANES), axis=0
    )
    head_grad[...] = jnp.concatenate([head[:, :channels], head[:, channels:]], axis=0)
    for o in range(members):
        for b in range(half_grid):
            if o == 0 and b == 0:

                @pl.when(jnp.logical_not(own_sum))
                def _():
                    sum_copy(0, 0).wait_send()

            else:
                sum_copy(o, b).wait_send()


def local(features, perturbation, target, head_weight, head_bias):
    members = lax.axis_size("member")
    grid_count = lax.axis_size("grid")
    _, band_rows, columns, hidden = features.shape
    channels = head_weight.shape[1]
    half = columns // 2
    cells = band_rows * half
    chips = members // 2
    head_rows = hidden // grid_count
    packed = head_rows // 2
    sum_dtype = BF16 if packed % 16 == 0 else F32
    dma = pltpu.SemaphoreType.DMA
    vmem = pl.BlockSpec(memory_space=pltpu.VMEM)
    hbm = pl.BlockSpec(memory_space=pl.ANY)
    return pl.pallas_call(
        functools.partial(kernel, members, grid_count),
        out_shape=(
            pltpu.VMEM(features.shape, BF16),
            pltpu.VMEM((head_rows, channels), F32),
        ),
        in_specs=[hbm, hbm, hbm, hbm, hbm],
        out_specs=(vmem, vmem),
        scratch_shapes=[
            pltpu.VMEM((channels, hidden), BF16),
            pltpu.VMEM((1, channels), F32),
            pltpu.VMEM((band_rows, columns, hidden), BF16),
            pltpu.VMEM((band_rows, columns, hidden), BF16),
            pltpu.VMEM(target.shape, BF16),
            pltpu.VMEM((band_rows * half, LANES), F32),
            pltpu.VMEM((2, 2 * channels, hidden), BF16),
            pltpu.VMEM((2, hidden, 2 * channels), BF16),
            pltpu.VMEM((2, cells, hidden), BF16),
            pltpu.VMEM((cells, hidden), BF16),
            pltpu.VMEM((2, cells, hidden), F32),
            pltpu.VMEM((chips, 2, cells, LANES), BF16),
            pltpu.VMEM((channels, hidden // 2), F32),
            pltpu.VMEM((grid_count // 2, packed, LANES), sum_dtype),
            pltpu.VMEM((chips, grid_count, packed, LANES), sum_dtype),
            dma((2, CHUNKS)),
            dma((2,)),
            dma,
            dma((chips, 2, CHUNKS)),
            dma((chips, 2, CHUNKS)),
            dma((CHUNKS,)),
            dma((CHUNKS,)),
            dma((members, grid_count // 2)),
            dma((chips, grid_count)),
        ],
        compiler_params=pltpu.CompilerParams(
            collective_id=0, has_side_effects=True, vmem_limit_bytes=56 * 1024 * 1024
        ),
        cost_estimate=pl.CostEstimate(
            flops=6 * band_rows * columns * hidden * channels,
            bytes_accessed=7 * band_rows * columns * hidden,
            transcendentals=2 * band_rows * columns * hidden,
        ),
    )(features, perturbation, target, head_weight.T, head_bias[None])


def solution(mesh):
    return jax.shard_map(
        local,
        mesh=mesh,
        in_specs=(
            P("member", None, "grid", None),
            P("member", None, "grid", None),
            P(None, "grid"),
            P(),
            P(),
        ),
        out_specs=(P("member", None, "grid", None), P("grid", None)),
        check_vma=False,
    )
```
